32 devices in a mesh: feed: 2 (over y), blk: 4 (over z), grp: 2 (over x), sub: 2 (over core).
Axes of the slice: x: 2, y: 2, z: 4, core: 2. Of those that a mesh axis runs over, the one named last changes fastest.
Arguments:
- embeddings: bfloat16 [16384, 1152], P(('feed', 'blk', 'grp', 'sub')), parts along dimension 0, may hold values from -6 to 6
- multipliers: bfloat16 [8192, 1024], P(('blk', 'grp', 'sub')), may hold values from -6 to 6
- labels: int32 [16384], P(('feed', 'blk', 'grp', 'sub')), parts along dimension 0, may hold values from 0 to 1, as said below
- spread: float32 [2], P('feed'), parts along dimension 0, may hold values from 0.06 to 0.12
Outputs:
- bootstrap: float32 [2048], P('feed'), parts along dimension 0
- statistic: float32 [2], P('feed'), parts along dimension 0
The draws below stay inside these ranges and needn't reach their ends.
There are 2 independent parts, one for each index of `feed`. The reference program is written for one: setup_inputs(seed, part) draws one part's arguments, and reference() takes and returns one part's arrays. A program takes and returns all parts, laid end to end along the dimension named above; an argument that names none is the same for every part. Nothing has to cross between parts.
Inputs may be any that keep to these rules, and one draw needn't show every extreme that they name: `labels`: in every feed row 0 is labelled 0 and the last row 1.
All inputs are finite; a program needn't handle non-finite values.
Results may differ from the reference program's by a relative error of at most 0.0054.
Values may be sent and summed in bfloat16 or wider, within the bound.
A program may use at most 64 MiB of HBM per device.

```python
import math
import jax
import jax.numpy as jnp
from jax import lax

D = 1152
MULT = 1024
R = 512
CP = 48
ROWS = 8192
N_BLK = 4
N_GRP = 2
N_SUB = 2


def draw_labels(key, part):
    key = jax.random.fold_in(key, 7)
    random_bits = jax.random.randint(key, (ROWS,), 0, 65536, dtype=jnp.int32)
    positions = jnp.arange(ROWS, dtype=jnp.int32)
    threshold = 16384 + positions // 64 * 32768 // max(ROWS // 64, 1)
    member = jnp.where(random_bits < threshold, 1, 0).astype(jnp.int32)
    member = member.at[0].set(0).at[ROWS - 1].set(1)
    return member


def block_scale(own_key, extent, split, smallest, top_value):
    def one(axis_at, parts):
        draws = jax.random.uniform(jax.random.fold_in(jax.random.fold_in(own_key, 6), axis_at), (parts,), jnp.float32, smallest / len(split), top_value / len(split))
        return jnp.repeat(jnp.exp(draws), extent[axis_at] // parts).reshape((-1,) + (1,) * (len(extent) - axis_at - 1))

    gain = one(*split[0])
    for cut in split[1:]:
        gain = gain * one(*cut)
    return gain


def noise(stream_key, extent, width, bound, cuts=(), held_as=jnp.bfloat16):
    result = jax.random.normal(stream_key, extent, jnp.float32) * width
    if len(cuts) > 0:
        result = block_scale(stream_key, extent, cuts, -0.22, 0.18) * result
    return jnp.clip(result, min=-bound, max=bound).astype(held_as)


def setup_inputs(seed: int = 0, part: int = 0) -> dict:
    keys = jax.random.split(jax.random.key(seed), 5)
    part_splits = jax.random.split(jax.random.fold_in(keys[4], part), 5)
    return {
        "embeddings": noise(part_splits[0], (ROWS, D), 1.0, 6.0, ((0, 16),)),
        "multipliers": noise(keys[1], (ROWS, MULT), 1.0, 6.0, ((0, 16),)),
        "labels": draw_labels(jax.random.fold_in(jax.random.fold_in(keys[4], part), 71), part),
        "spread": jnp.clip(jnp.exp(jax.random.uniform(part_splits[3], (1,), jnp.float32, math.log(0.06), math.log(0.12))), 0.06, 0.12),
    }


def reference(embeddings, multipliers, labels, spread):
    floats = embeddings.astype(jnp.float32)
    unit_rows = (floats / jnp.sqrt(lax.optimization_barrier(jnp.sum(floats * floats, axis=1, keepdims=True)) + 1e-06)).astype(jnp.bfloat16)
    row_total = jnp.float32(ROWS)
    ones_all = jnp.sum(labels.astype(jnp.float32))
    weights = jnp.where(labels == 1, -row_total / (2.0 * ones_all), row_total / (2.0 * (row_total - ones_all)))
    scaled = (multipliers.astype(jnp.float32) * weights[:, None]).astype(jnp.bfloat16)
    signs = weights.astype(jnp.bfloat16)
    group_size = N_GRP * N_SUB
    block_rows = group_size * R
    part_unit = unit_rows.reshape(N_BLK, group_size, R, D)[:, :, :CP, :].reshape(N_BLK, group_size * CP, D)
    part_scaled = scaled.reshape(N_BLK, group_size, R, MULT)[:, :, :CP, :].reshape(N_BLK, group_size * CP, MULT)
    part_signs = signs.reshape(N_BLK, group_size, R)[:, :, :CP].reshape(N_BLK, group_size * CP)
    positions = jnp.arange(block_rows, dtype=jnp.int32)
    within = positions % R
    row_key = jnp.where(within < CP, positions // R * CP + within, -1)
    col_key = jnp.arange(group_size * CP, dtype=jnp.int32)
    own_mask = row_key[:, None] == col_key[None, :]
    band_width = spread[0]

    def one_block(block_index):
        offset = block_index * block_rows
        rows_unit = lax.dynamic_slice_in_dim(unit_rows, offset, block_rows, 0)
        rows_scaled = lax.dynamic_slice_in_dim(scaled, offset, block_rows, 0)
        rows_weights = lax.dynamic_slice_in_dim(weights, offset, block_rows, 0)
        previous = (block_index + N_BLK - 1) % N_BLK
        boot_sum = jnp.zeros((MULT,), jnp.float32)
        stat_sum = jnp.zeros((), jnp.float32)
        for partner_index, masked in ((block_index, True), (previous, False)):
            cols_unit = lax.dynamic_index_in_dim(part_unit, partner_index, 0, keepdims=False)
            cols_scaled = lax.dynamic_index_in_dim(part_scaled, partner_index, 0, keepdims=False)
            cols_signs = lax.dynamic_index_in_dim(part_signs, partner_index, 0, keepdims=False)
            scores = jnp.dot(rows_unit, cols_unit.T, preferred_element_type=jnp.float32)
            kernel = jnp.exp(scores / band_width)
            if masked:
                kernel = jnp.where(own_mask, 0.0, kernel)
            kernel_low = kernel.astype(jnp.bfloat16)
            mixed_rows = jnp.dot(kernel_low, cols_scaled, preferred_element_type=jnp.float32)
            boot_sum = boot_sum + lax.optimization_barrier(jnp.sum(rows_scaled.astype(jnp.float32) * mixed_rows, axis=0))
            stat_sum = stat_sum + jnp.sum(rows_weights * jnp.dot(kernel_low, cols_signs, preferred_element_type=jnp.float32))
        return (boot_sum, stat_sum)
    boots, stats = lax.map(one_block, jnp.arange(N_BLK, dtype=jnp.int32))
    normalizer = 1.0 / math.sqrt(ROWS * 2 * group_size * CP)
    return (lax.optimization_barrier(jnp.sum(boots, axis=0)) * normalizer, jnp.reshape(jnp.sum(stats) * normalizer, (1,)))
```

```python
import functools
import math

import jax
import jax.numpy as jnp
from jax import lax
from jax.experimental import pallas as pl
from jax.experimental.pallas import tpu as pltpu
from jax.sharding import PartitionSpec as P

CP = 48
LANES = 128
MESH = pl.DeviceIdType.MESH


def column(row, rows):
    return jnp.broadcast_to(row, (LANES, LANES)).T[:rows]


def wide(tile, width):
    return jnp.concatenate([tile] * (width // LANES), axis=1)


def kernel(
    n_blk, n_grp, n_sub, spread_ref, lab_hbm, emb_hbm, mul_hbm, boot_ref, stat_ref,
    emb, mul, unit, scaled, u_own, u_prev, m_own, m_prev, lab, w_part, red,
    load_sem, lab_send, lab_recv, red_send, red_recv,
    x_send, x_recv, z_send, z_recv, f_send, f_recv, s_send, s_recv,
):
    feed, blk = lax.axis_index("feed"), lax.axis_index("blk")
    grp, sub = lax.axis_index("grp"), lax.axis_index("sub")
    group = n_grp * n_sub
    n = n_blk * group
    slot = grp * n_sub + sub
    me = blk * group + slot
    rows, width = emb.shape
    cols = mul.shape[1]
    row_total = float(n * rows)
    small = n <= 16
    nxt = lax.rem(blk + 1, n_blk)
    prv = lax.rem(blk + n_blk - 1, n_blk)

    def peer(k):
        p = lax.rem(me + k, n)
        b, r = p // group, lax.rem(p, group)
        return (feed, b, r // n_sub, lax.rem(r, n_sub))

    def others(do):
        def step(k, c):
            do(peer(k))
            return c
        lax.fori_loop(1, n, step, 0, unroll=small)

    head_e = pltpu.make_async_copy(emb_hbm.at[pl.ds(0, CP)], emb.at[pl.ds(0, CP)], load_sem.at[0])
    head_m = pltpu.make_async_copy(mul_hbm.at[pl.ds(0, CP)], m_own.at[slot], load_sem.at[1])
    rest_e = pltpu.make_async_copy(
        emb_hbm.at[pl.ds(CP, rows - CP)], emb.at[pl.ds(CP, rows - CP)], load_sem.at[2])
    load_m = pltpu.make_async_copy(mul_hbm, mul, load_sem.at[3])
    load_l = pltpu.make_async_copy(lab_hbm, lab.at[me], load_sem.at[4])
    for c in (head_e, head_m, load_l, rest_e, load_m):
        c.start()

    barrier = pltpu.get_barrier_semaphore()
    others(lambda d: pl.semaphore_signal(barrier, inc=1, device_id=d, device_id_type=MESH))

    def normalise(lo, count):
        x = emb[pl.ds(lo, count), :].astype(jnp.float32)
        inv = lax.rsqrt(jnp.sum(x * x, axis=1, keepdims=True) + 1e-06)
        return (x * inv).astype(jnp.bfloat16)

    head_e.wait()
    head = normalise(0, CP)
    u_own[slot] = head
    unit[pl.ds(0, CP), :] = head
    head_m.wait()
    load_l.wait()
    pl.semaphore_wait(barrier, n - 1)

    def remote(src, dst, send, recv, dev):
        return pltpu.make_async_remote_copy(
            src_ref=src, dst_ref=dst, send_sem=send, recv_sem=recv, device_id=dev, device_id_type=MESH)

    own = (u_own, m_own)
    prev = (u_prev, m_prev)

    def x_copy(what, hop):
        return remote(own[what].at[slot], own[what].at[slot], x_send.at[what, hop], x_recv.at[what, hop],
                      (feed, blk, lax.rem(grp + hop, n_grp), sub))

    def z_copy(what):
        return remote(own[what].at[slot], prev[what].at[slot], z_send.at[what], z_recv.at[what],
                      (feed, nxt, grp, sub))

    def behind(hop):
        return lax.rem(grp + n_grp - hop, n_grp)

    def z_pass(hop):
        at = behind(hop) * n_sub + sub
        return remote(u_own.at[at], u_prev.at[at], f_send.at[0, hop], f_recv.at[0, hop],
                      (feed, nxt, grp, sub))

    def x_pass(hop):
        return remote(m_prev.at[slot], m_prev.at[slot], f_send.at[1, hop], f_recv.at[1, hop],
                      (feed, blk, lax.rem(grp + hop, n_grp), sub))

    def sib(ref, kind, hop, by):
        at = behind(hop) * n_sub + sub
        return remote(ref.at[at], ref.at[at], s_send.at[kind, hop, by], s_recv.at[kind, hop, by],
                      (feed, blk, grp, lax.rem(sub + by, n_sub)))

    started = []

    def go(c):
        c.start()
        started.append(c)

    refs = (u_own, m_own, u_prev, m_prev)

    def to_sib(kind, hop):
        for by in range(1, n_sub):
            go(sib(refs[kind], kind, hop, by))

    def from_sib(kind):
        for hop in range(n_grp):
            for by in range(1, n_sub):
                sib(refs[kind], kind, hop, by).wait_recv()

    hops = range(1, n_grp)
    for hop in hops:
        go(x_copy(0, hop))
    go(z_copy(0))
    to_sib(0, 0)
    others(lambda d: remote(lab.at[me], lab.at[me], lab_send, lab_recv, d).start())
    for hop in hops:
        go(x_copy(1, hop))
    go(z_copy(1))
    to_sib(1, 0)

    rest_e.wait()
    step = 16 * ((rows - CP) // 64)
    for lo in range(CP, rows, step):
        count = min(step, rows - lo)
        unit[pl.ds(lo, count), :] = normalise(lo, count)

    pltpu.make_async_copy(lab.at[pl.ds(0, n - 1)], lab.at[pl.ds(0, n - 1)], lab_recv).wait()
    ones = jnp.sum(jnp.sum(lab[...].astype(jnp.float32), axis=0), keepdims=True)
    ones = jnp.broadcast_to(jnp.reshape(ones, (1, 1)), (1, LANES))
    w_one = -row_total / (2.0 * ones)
    w_zero = row_total / (2.0 * (row_total - ones))

    def weigh(row):
        return jnp.where(row == 1, w_one, w_zero)

    def part_weights(base, owner):
        def one(k, c):
            row = weigh(lab[owner * group + k, 0:1, :])
            w_part[base + k] = column(row, CP)
            return c
        lax.fori_loop(0, group, one, 0, unroll=small)

    load_m.wait()
    w_rows = []
    for c in range(rows // LANES):
        row = weigh(lab[me, c : c + 1, :])
        w_rows.append(row)
        here = pl.ds(c * LANES, LANES)
        scaled[here, :] = (mul[here, :].astype(jnp.float32) * wide(column(row, LANES), cols)).astype(jnp.bfloat16)
    part_weights(0, blk)
    part_weights(group, prv)

    inv_band = 1.0 / jnp.full((1, LANES), spread_ref[0], jnp.float32)
    per = math.gcd(group, 4)
    take = per * CP

    def pairs(u_ref, m_ref, base, masked, first):
        def chunk(t, carry):
            boots, stat = carry
            some = pl.ds(t * per, per)
            u = u_ref[some].reshape(take, width)
            scores = lax.dot_general(u, unit[...], (((1,), (1,)), ((), ())), preferred_element_type=jnp.float32)
            kern = jnp.exp(scores * wide(inv_band, rows))
            if masked:
                at = lax.broadcasted_iota(jnp.int32, kern.shape, 0) + (t * per - slot) * CP
                lane = lax.broadcasted_iota(jnp.int32, kern.shape, 1)
                kern = jnp.where((at == lane) & (lane < CP), 0.0, kern)
            low = kern.astype(jnp.bfloat16)
            back = low.astype(jnp.float32)
            w = w_part[pl.ds(base + t * per, per)].reshape(take, LANES)
            signs = w.astype(jnp.bfloat16).astype(jnp.float32)
            total = back[:, :LANES] * w_rows[0]
            for c in range(1, rows // LANES):
                total = total + back[:, c * LANES : (c + 1) * LANES] * w_rows[c]
            stat = stat + jnp.sum(total * signs, axis=0, keepdims=True)
            new = []
            wide_cols = 2 * LANES
            for c in range(cols // wide_cols):
                here = pl.ds(c * wide_cols, wide_cols)
                mixed = jnp.dot(low, scaled[:, here], preferred_element_type=jnp.float32)
                m = m_ref[some, :, here].reshape(take, wide_cols).astype(jnp.float32)
                sc = (m * wide(w, wide_cols)).astype(jnp.bfloat16).astype(jnp.float32)
                new.append(boots[c] + jnp.sum(sc * mixed, axis=0, keepdims=True))
            return tuple(new), stat

        count = group // per
        if count == 1:
            return chunk(0, first)
        return lax.fori_loop(0, count, chunk, first)

    for hop in hops:
        x_copy(0, hop).wait_recv()
        go(z_pass(hop))
        to_sib(0, hop)
    z_copy(0).wait_recv()
    to_sib(2, 0)
    z_copy(1).wait_recv()
    for hop in hops:
        go(x_pass(hop))
    to_sib(3, 0)
    for hop in hops:
        x_copy(1, hop).wait_recv()
        to_sib(1, hop)

    zero = (tuple(jnp.zeros((1, 2 * LANES), jnp.float32) for _ in range(cols // (2 * LANES))),
            jnp.zeros((1, LANES), jnp.float32))
    from_sib(0)
    from_sib(1)
    acc = pairs(u_own, m_own, 0, True, zero)
    for hop in hops:
        z_pass(hop).wait_recv()
        to_sib(2, hop)
    for hop in hops:
        x_pass(hop).wait_recv()
        to_sib(3, hop)
    from_sib(2)
    from_sib(3)
    boots, stat = pairs(u_prev, m_prev, group, False, acc)

    for c, b in enumerate(boots):
        red[me, 2 * c : 2 * c + 1, :] = b[:, :LANES]
        red[me, 2 * c + 1 : 2 * c + 2, :] = b[:, LANES:]
    tiles = cols // LANES
    red[me, tiles : tiles + 1, :] = stat
    others(lambda d: remote(red.at[me], red.at[me], red_send, red_recv, d).start())
    for c in started:
        c.wait_send()
    pltpu.make_async_copy(lab.at[pl.ds(0, n - 1)], lab.at[pl.ds(0, n - 1)], lab_send).wait()
    pltpu.make_async_copy(red.at[pl.ds(0, n - 1)], red.at[pl.ds(0, n - 1)], red_recv).wait()
    normalizer = 1.0 / math.sqrt(row_total * 2 * group * CP)
    total = jnp.sum(red[...], axis=0) * normalizer
    boot_ref[...] = total[:tiles]
    stat_ref[...] = jnp.sum(total[tiles : tiles + 1], axis=1, keepdims=True)
    pltpu.make_async_copy(red.at[pl.ds(0, n - 1)], red.at[pl.ds(0, n - 1)], red_send).wait()


def body(sizes, embeddings, multipliers, labels, spread):
    n_blk, n_grp, n_sub = sizes
    group = n_grp * n_sub
    n = n_blk * group
    rows, width = embeddings.shape
    cols = multipliers.shape[1]
    bf16, f32 = jnp.bfloat16, jnp.float32
    dma = pltpu.SemaphoreType.DMA
    boot, stat = pl.pallas_call(
        functools.partial(kernel, n_blk, n_grp, n_sub),
        out_shape=(
            jax.ShapeDtypeStruct((cols // LANES, LANES), f32),
            jax.ShapeDtypeStruct((1, 1), f32),
        ),
        in_specs=[
            pl.BlockSpec(memory_space=pltpu.SMEM),
            pl.BlockSpec(memory_space=pl.ANY),
            pl.BlockSpec(memory_space=pl.ANY),
            pl.BlockSpec(memory_space=pl.ANY),
        ],
        out_specs=(pl.BlockSpec(memory_space=pltpu.VMEM), pl.BlockSpec(memory_space=pltpu.VMEM)),
        scratch_shapes=[
            pltpu.VMEM((rows, width), bf16),
            pltpu.VMEM((rows, cols), bf16),
            pltpu.VMEM((rows, width), bf16),
            pltpu.VMEM((rows, cols), bf16),
            pltpu.VMEM((group, CP, width), bf16),
            pltpu.VMEM((group, CP, width), bf16),
            pltpu.VMEM((group, CP, cols), bf16),
            pltpu.VMEM((group, CP, cols), bf16),
            pltpu.VMEM((n, rows // LANES, LANES), jnp.int32),
            pltpu.VMEM((2 * group, CP, LANES), f32),
            pltpu.VMEM((n, cols // LANES + 1, LANES), f32),
            dma((5,)), dma, dma, dma, dma,
            dma((2, n_grp)), dma((2, n_grp)), dma((2,)), dma((2,)),
            dma((2, n_grp)), dma((2, n_grp)), dma((4, n_grp, n_sub)), dma((4, n_grp, n_sub)),
        ],
        compiler_params=pltpu.CompilerParams(
            collective_id=0, has_side_effects=True, vmem_limit_bytes=48 * 1024 * 1024
        ),
        name="bootstrap",
    )(spread, labels.reshape(rows // LANES, LANES), embeddings, multipliers)
    return boot.reshape(cols), stat.reshape(1)


def solution(mesh):
    placed = (
        P(("feed", "blk", "grp", "sub"), None),
        P(("blk", "grp", "sub"), None),
        P(("feed", "blk", "grp", "sub")),
        P("feed"),
    )
    sizes = (mesh.shape["blk"], mesh.shape["grp"], mesh.shape["sub"])
    return jax.shard_map(
        functools.partial(body, sizes), mesh=mesh, in_specs=placed, out_specs=(P("feed"), P("feed")),
        check_vma=False,
    )
```

```python
import functools
import math

import jax
import jax.numpy as jnp
from jax import lax
from jax.experimental import pallas as pl
from jax.experimental.pallas import tpu as pltpu
from jax.sharding import PartitionSpec as P

CP = 48
LANES = 128
MESH = pl.DeviceIdType.MESH


def column(row, rows):
    return jnp.broadcast_to(row, (LANES, LANES)).T[:rows]


def wide(tile, width):
    return jnp.concatenate([tile] * (width // LANES), axis=1)


def kernel(
    n_blk, n_grp, n_sub, spread_ref, lab_hbm, emb_hbm, mul_hbm, red,
    emb, mul, unit, scaled, u_own, u_prev, m_own, m_prev, lab, w_part,
    load_sem, lab_send, lab_recv, red_send, red_recv,
    x_send, x_recv, z_send, z_recv, f_send, f_recv, s_send, s_recv, spread_v,
):
    feed, blk = lax.axis_index("feed"), lax.axis_index("blk")
    grp, sub = lax.axis_index("grp"), lax.axis_index("sub")
    group = n_grp * n_sub
    n = n_blk * group
    slot = grp * n_sub + sub
    me = blk * group + slot
    rows, width = emb.shape
    cols = mul.shape[1]
    row_total = float(n * rows)
    small = n <= 16
    nxt = lax.rem(blk + 1, n_blk)
    prv = lax.rem(blk + n_blk - 1, n_blk)

    def peer(k):
        p = lax.rem(me + k, n)
        b, r = p // group, lax.rem(p, group)
        return (feed, b, r // n_sub, lax.rem(r, n_sub))

    def others(do):
        def step(k, c):
            do(peer(k))
            return c
        lax.fori_loop(1, n, step, 0, unroll=small)

    head_e = pltpu.make_async_copy(emb_hbm.at[pl.ds(0, CP)], emb.at[pl.ds(0, CP)], load_sem.at[0])
    head_m = pltpu.make_async_copy(mul_hbm.at[pl.ds(0, CP)], m_own.at[slot], load_sem.at[1])
    rest_e = pltpu.make_async_copy(
        emb_hbm.at[pl.ds(CP, rows - CP)], emb.at[pl.ds(CP, rows - CP)], load_sem.at[2])
    load_m = pltpu.make_async_copy(mul_hbm, mul, load_sem.at[3])
    load_l = pltpu.make_async_copy(lab_hbm, lab.at[me], load_sem.at[4])
    load_s = pltpu.make_async_copy(spread_ref, spread_v, load_sem.at[5])
    for c in (head_e, head_m, load_l, load_s, rest_e, load_m):
        c.start()

    barrier = pltpu.get_barrier_semaphore()
    others(lambda d: pl.semaphore_signal(barrier, inc=1, device_id=d, device_id_type=MESH))

    def normalise(lo, count):
        x = emb[pl.ds(lo, count), :].astype(jnp.float32)
        inv = lax.rsqrt(jnp.sum(x * x, axis=1, keepdims=True) + 1e-06)
        return (x * inv).astype(jnp.bfloat16)

    head_e.wait()
    head = normalise(0, CP)
    u_own[slot] = head
    unit[pl.ds(0, CP), :] = head
    head_m.wait()
    load_l.wait()
    pl.semaphore_wait(barrier, n - 1)

    def remote(src, dst, send, recv, dev):
        return pltpu.make_async_remote_copy(
            src_ref=src, dst_ref=dst, send_sem=send, recv_sem=recv, device_id=dev, device_id_type=MESH)

    own = (u_own, m_own)
    prev = (u_prev, m_prev)

    def x_copy(what, hop):
        return remote(own[what].at[slot], own[what].at[slot], x_send.at[what, hop], x_recv.at[what, hop],
                      (feed, blk, lax.rem(grp + hop, n_grp), sub))

    def z_copy(what):
        return remote(own[what].at[slot], prev[what].at[slot], z_send.at[what], z_recv.at[what],
                      (feed, nxt, grp, sub))

    def behind(hop):
        return lax.rem(grp + n_grp - hop, n_grp)

    def z_pass(hop):
        at = behind(hop) * n_sub + sub
        return remote(u_own.at[at], u_prev.at[at], f_send.at[0, hop], f_recv.at[0, hop],
                      (feed, nxt, grp, sub))

    def x_pass(hop):
        return remote(m_prev.at[slot], m_prev.at[slot], f_send.at[1, hop], f_recv.at[1, hop],
                      (feed, blk, lax.rem(grp + hop, n_grp), sub))

    def sib(ref, kind, hop, by):
        at = behind(hop) * n_sub + sub
        return remote(ref.at[at], ref.at[at], s_send.at[kind, hop, by], s_recv.at[kind, hop, by],
                      (feed, blk, grp, lax.rem(sub + by, n_sub)))

    started = []

    def go(c):
        c.start()
        started.append(c)

    refs = (u_own, m_own, u_prev, m_prev)

    def to_sib(kind, hop):
        for by in range(1, n_sub):
            go(sib(refs[kind], kind, hop, by))

    def from_sib(kind):
        for hop in range(n_grp):
            for by in range(1, n_sub):
                sib(refs[kind], kind, hop, by).wait_recv()

    hops = range(1, n_grp)
    others(lambda d: remote(lab.at[me], lab.at[me], lab_send, lab_recv, d).start())
    for hop in hops:
        go(x_copy(0, hop))
    go(z_copy(0))
    to_sib(0, 0)
    for hop in hops:
        go(x_copy(1, hop))
    go(z_copy(1))
    to_sib(1, 0)

    rest_e.wait()
    step = 16 * ((rows - CP) // 64)
    for lo in range(CP, rows, step):
        count = min(step, rows - lo)
        unit[pl.ds(lo, count), :] = normalise(lo, count)

    for hop in hops:
        x_copy(0, hop).wait_recv()
        go(z_pass(hop))
        to_sib(0, hop)
    z_copy(0).wait_recv()
    to_sib(2, 0)
    z_copy(1).wait_recv()
    for hop in hops:
        go(x_pass(hop))
    to_sib(3, 0)
    for hop in hops:
        x_copy(1, hop).wait_recv()
        to_sib(1, hop)

    pltpu.make_async_copy(lab.at[pl.ds(0, n - 1)], lab.at[pl.ds(0, n - 1)], lab_recv).wait()
    ones = jnp.sum(jnp.sum(lab[...].astype(jnp.float32), axis=0), keepdims=True)
    ones = jnp.broadcast_to(jnp.reshape(ones, (1, 1)), (1, LANES))
    w_one = -row_total / (2.0 * ones)
    w_zero = row_total / (2.0 * (row_total - ones))

    def weigh(row):
        return jnp.where(row == 1, w_one, w_zero)

    def part_weights(base, owner):
        def one(k, c):
            row = weigh(lab[owner * group + k, 0:1, :])
            w_part[base + k] = column(row, CP)
            return c
        lax.fori_loop(0, group, one, 0, unroll=small)

    load_m.wait()
    load_s.wait()
    w_rows = []
    for c in range(rows // LANES):
        row = weigh(lab[me, c : c + 1, :])
        w_rows.append(row)
        here = pl.ds(c * LANES, LANES)
        scaled[here, :] = (mul[here, :].astype(jnp.float32) * wide(column(row, LANES), cols)).astype(jnp.bfloat16)
    part_weights(0, blk)
    part_weights(group, prv)

    inv_band = 1.0 / jnp.broadcast_to(spread_v[...], (1, LANES))
    per = math.gcd(group, 4)
    take = per * CP

    def pairs(u_ref, m_ref, base, masked, first):
        def chunk(t, carry):
            boots, stat = carry
            some = pl.ds(t * per, per)
            u = u_ref[some].reshape(take, width)
            scores = lax.dot_general(u, unit[...], (((1,), (1,)), ((), ())), preferred_element_type=jnp.float32)
            kern = jnp.exp(scores * wide(inv_band, rows))
            if masked:
                at = lax.broadcasted_iota(jnp.int32, kern.shape, 0) + (t * per - slot) * CP
                lane = lax.broadcasted_iota(jnp.int32, kern.shape, 1)
                kern = jnp.where((at == lane) & (lane < CP), 0.0, kern)
            low = kern.astype(jnp.bfloat16)
            back = low.astype(jnp.float32)
            w = w_part[pl.ds(base + t * per, per)].reshape(take, LANES)
            signs = w.astype(jnp.bfloat16).astype(jnp.float32)
            total = back[:, :LANES] * w_rows[0]
            for c in range(1, rows // LANES):
                total = total + back[:, c * LANES : (c + 1) * LANES] * w_rows[c]
            stat = stat + jnp.sum(total * signs, axis=0, keepdims=True)
            new = []
            wide_cols = 2 * LANES
            for c in range(cols // wide_cols):
                here = pl.ds(c * wide_cols, wide_cols)
                mixed = jnp.dot(low, scaled[:, here], preferred_element_type=jnp.float32)
                m = m_ref[some, :, here].reshape(take, wide_cols).astype(jnp.float32)
                sc = (m * wide(w, wide_cols)).astype(jnp.bfloat16).astype(jnp.float32)
                new.append(boots[c] + jnp.sum(sc * mixed, axis=0, keepdims=True))
            return tuple(new), stat

        count = group // per
        if count == 1:
            return chunk(0, first)
        return lax.fori_loop(0, count, chunk, first)

    zero = (tuple(jnp.zeros((1, 2 * LANES), jnp.float32) for _ in range(cols // (2 * LANES))),
            jnp.zeros((1, LANES), jnp.float32))
    from_sib(0)
    from_sib(1)
    acc = pairs(u_own, m_own, 0, True, zero)
    for hop in hops:
        z_pass(hop).wait_recv()
        to_sib(2, hop)
    for hop in hops:
        x_pass(hop).wait_recv()
        to_sib(3, hop)
    from_sib(2)
    from_sib(3)
    boots, stat = pairs(u_prev, m_prev, group, False, acc)

    for c, b in enumerate(boots):
        red[me, 2 * c : 2 * c + 1, :] = b[:, :LANES]
        red[me, 2 * c + 1 : 2 * c + 2, :] = b[:, LANES:]
    tiles = cols // LANES
    red[me, tiles : tiles + 1, :] = stat
    others(lambda d: remote(red.at[me], red.at[me], red_send, red_recv, d).start())
    for c in started:
        c.wait_send()
    pltpu.make_async_copy(lab.at[pl.ds(0, n - 1)], lab.at[pl.ds(0, n - 1)], lab_send).wait()
    pltpu.make_async_copy(red.at[pl.ds(0, n - 1)], red.at[pl.ds(0, n - 1)], red_recv).wait()
    pltpu.make_async_copy(red.at[pl.ds(0, n - 1)], red.at[pl.ds(0, n - 1)], red_send).wait()


def close(normalizer, red, boot_ref, stat_ref):
    total = jnp.sum(red[...], axis=0) * normalizer
    tiles = total.shape[0] - 1
    boot_ref[...] = total[:tiles]
    stat_ref[...] = jnp.sum(total[tiles:], axis=1, keepdims=True)


def body(sizes, embeddings, multipliers, labels, spread):
    n_blk, n_grp, n_sub = sizes
    group = n_grp * n_sub
    n = n_blk * group
    rows, width = embeddings.shape
    cols = multipliers.shape[1]
    bf16, f32 = jnp.bfloat16, jnp.float32
    dma = pltpu.SemaphoreType.DMA
    red = pl.pallas_call(
        functools.partial(kernel, n_blk, n_grp, n_sub),
        out_shape=jax.ShapeDtypeStruct((n, cols // LANES + 1, LANES), f32),
        in_specs=[
            pl.BlockSpec(memory_space=pl.ANY),
            pl.BlockSpec(memory_space=pl.ANY),
            pl.BlockSpec(memory_space=pl.ANY),
            pl.BlockSpec(memory_space=pl.ANY),
        ],
        out_specs=pl.BlockSpec(memory_space=pltpu.VMEM),
        scratch_shapes=[
            pltpu.VMEM((rows, width), bf16),
            pltpu.VMEM((rows, cols), bf16),
            pltpu.VMEM((rows, width), bf16),
            pltpu.VMEM((rows, cols), bf16),
            pltpu.VMEM((group, CP, width), bf16),
            pltpu.VMEM((group, CP, width), bf16),
            pltpu.VMEM((group, CP, cols), bf16),
            pltpu.VMEM((group, CP, cols), bf16),
            pltpu.VMEM((n, rows // LANES, LANES), jnp.int32),
            pltpu.VMEM((2 * group, CP, LANES), f32),
            dma((6,)), dma, dma, dma, dma,
            dma((2, n_grp)), dma((2, n_grp)), dma((2,)), dma((2,)),
            dma((2, n_grp)), dma((2, n_grp)), dma((4, n_grp, n_sub)), dma((4, n_grp, n_sub)), pltpu.VMEM((1, 1), f32),
        ],
        compiler_params=pltpu.CompilerParams(
            collective_id=0, has_side_effects=True, vmem_limit_bytes=63 * 1024 * 1024
        ),
        name="bootstrap",
    )(spread.reshape(1, 1), labels.reshape(rows // LANES, LANES), embeddings, multipliers)
    normalizer = 1.0 / math.sqrt(float(n * rows) * 2 * group * CP)
    boot, stat = pl.pallas_call(
        functools.partial(close, normalizer),
        out_shape=(
            jax.ShapeDtypeStruct((cols // LANES, LANES), f32),
            jax.ShapeDtypeStruct((1, 1), f32),
        ),
        in_specs=[pl.BlockSpec(memory_space=pltpu.VMEM)],
        out_specs=(pl.BlockSpec(memory_space=pltpu.VMEM), pl.BlockSpec(memory_space=pltpu.VMEM)),
        name="close",
    )(red)
    return boot.reshape(cols), stat.reshape(1)


def solution(mesh):
    placed = (
        P(("feed", "blk", "grp", "sub"), None),
        P(("blk", "grp", "sub"), None),
        P(("feed", "blk", "grp", "sub")),
        P("feed"),
    )
    sizes = (mesh.shape["blk"], mesh.shape["grp"], mesh.shape["sub"])
    return jax.shard_map(
        functools.partial(body, sizes), mesh=mesh, in_specs=placed, out_specs=(P("feed"), P("feed")),
        check_vma=False,
    )
```

```python
import functools
import math

import jax
import jax.numpy as jnp
from jax import lax
from jax.experimental import pallas as pl
from jax.experimental.pallas import tpu as pltpu
from jax.sharding import PartitionSpec as P

CP = 48
LANES = 128
PIECE = 48
MESH = pl.DeviceIdType.MESH


def column(row, rows):
    return jnp.broadcast_to(row, (LANES, LANES)).T[:rows]


def wide(tile, width):
    return jnp.concatenate([tile] * (width // LANES), axis=1)


def kernel(
    n_blk, n_grp, n_sub, spread_ref, lab_hbm, emb_hbm, mul_hbm, red,
    emb, mul, unit, scaled, u_own, u_prev, m_own, m_prev, lab, w_part,
    load_sem, lab_send, lab_recv, red_send, red_recv,
    x_send, x_recv, z_send, z_recv, f_send, f_recv, s_send, s_recv, spread_v,
):
    feed, blk = lax.axis_index("feed"), lax.axis_index("blk")
    grp, sub = lax.axis_index("grp"), lax.axis_index("sub")
    group = n_grp * n_sub
    n = n_blk * group
    slot = grp * n_sub + sub
    me = blk * group + slot
    rows, width = emb.shape
    cols = mul.shape[1]
    row_total = float(n * rows)
    small = n <= 16
    nxt = lax.rem(blk + 1, n_blk)
    prv = lax.rem(blk + n_blk - 1, n_blk)

    def others(do):
        up = blk < n_blk // 2

        def one(b, lo):
            for k in range(lo, group):
                r = lax.rem(slot + k, group)
                do((feed, b, r // n_sub, lax.rem(r, n_sub)))

        def step(k, c):
            b = jnp.where(up, n_blk - 1 - k, k)
            past = jnp.where(up, b <= blk, b >= blk)
            one(jnp.where(past, jnp.where(up, b - 1, b + 1), b), 0)
            return c

        lax.fori_loop(0, n_blk - 1, step, 0, unroll=small)
        one(blk, 1)

    head_e = pltpu.make_async_copy(emb_hbm.at[pl.ds(0, CP)], emb.at[pl.ds(0, CP)], load_sem.at[0])
    head_m = pltpu.make_async_copy(mul_hbm.at[pl.ds(0, CP)], m_own.at[slot], load_sem.at[1])
    rest_e = pltpu.make_async_copy(
        emb_hbm.at[pl.ds(CP, rows - CP)], emb.at[pl.ds(CP, rows - CP)], load_sem.at[2])
    load_m = pltpu.make_async_copy(mul_hbm, mul, load_sem.at[3])
    load_l = pltpu.make_async_copy(lab_hbm, lab.at[me], load_sem.at[4])
    load_s = pltpu.make_async_copy(spread_ref, spread_v, load_sem.at[5])
    for c in (head_e, head_m, load_l, load_s, rest_e, load_m):
        c.start()

    barrier = pltpu.get_barrier_semaphore()
    others(lambda d: pl.semaphore_signal(barrier, inc=1, device_id=d, device_id_type=MESH))

    def normalise(lo, count):
        x = emb[pl.ds(lo, count), :].astype(jnp.float32)
        inv = lax.rsqrt(jnp.sum(x * x, axis=1, keepdims=True) + 1e-06)
        return (x * inv).astype(jnp.bfloat16)

    load_l.wait()
    pl.semaphore_wait(barrier, n - 1)

    def remote(src, dst, send, recv, dev):
        return pltpu.make_async_remote_copy(
            src_ref=src, dst_ref=dst, send_sem=send, recv_sem=recv, device_id=dev, device_id_type=MESH)

    mul_head = mul_hbm.at[pl.ds(0, CP)]
    prev = (u_prev, m_prev)

    parts = CP // PIECE

    def piece(ref, at, c):
        return ref.at[at, pl.ds(c * PIECE, PIECE)]

    def x_copy(what, hop, c):
        src = piece(u_own, slot, c) if what == 0 else mul_head
        dst = piece(u_own, slot, c) if what == 0 else m_own.at[slot]
        return remote(src, dst, x_send.at[what, hop, c], x_recv.at[what, hop, c],
                      (feed, blk, lax.rem(grp + hop, n_grp), sub))

    def z_copy(what):
        return remote(u_own.at[slot] if what == 0 else mul_head, prev[what].at[slot], z_send.at[what], z_recv.at[what],
                      (feed, nxt, grp, sub))

    def behind(hop):
        return lax.rem(grp + n_grp - hop, n_grp)

    def z_pass(hop, c):
        at = behind(hop) * n_sub + sub
        return remote(piece(u_own, at, c), piece(u_prev, at, c), f_send.at[0, hop, c], f_recv.at[0, hop, c],
                      (feed, nxt, grp, sub))

    def x_pass(hop, c):
        return remote(m_prev.at[slot], m_prev.at[slot], f_send.at[1, hop, c], f_recv.at[1, hop, c],
                      (feed, blk, lax.rem(grp + hop, n_grp), sub))

    def sib(kind, hop, by, c):
        at = behind(hop) * n_sub + sub
        ref = refs[kind].at[at] if not split(kind, hop) else piece(refs[kind], at, c)
        return remote(ref, ref, s_send.at[kind, hop, by, c], s_recv.at[kind, hop, by, c],
                      (feed, blk, grp, lax.rem(sub + by, n_sub)))

    started = []

    def go(c):
        c.start()
        started.append(c)

    refs = (u_own, m_own, u_prev, m_prev)

    def split(kind, hop):
        return kind == 2 and hop > 0

    def to_sib(kind, hop, c=0):
        for by in range(1, n_sub):
            go(sib(kind, hop, by, c))

    def from_sib(kind):
        for hop in range(n_grp):
            for by in range(1, n_sub):
                for c in range(parts if split(kind, hop) else 1):
                    sib(kind, hop, by, c).wait_recv()

    hops = range(1, n_grp)
    go(z_copy(1))
    others(lambda d: remote(lab.at[me], lab.at[me], lab_send, lab_recv, d).start())
    head_e.wait()
    head = normalise(0, CP)
    u_own[slot] = head
    unit[pl.ds(0, CP), :] = head
    for c in range(parts):
        for hop in hops:
            go(x_copy(0, hop, c))
    go(z_copy(0))
    to_sib(0, 0)
    for hop in hops:
        go(x_copy(1, hop, 0))
    head_m.wait()
    to_sib(1, 0)

    rest_e.wait()
    step = 16 * ((rows - CP) // 64)
    for lo in range(CP, rows, step):
        count = min(step, rows - lo)
        unit[pl.ds(lo, count), :] = normalise(lo, count)

    for c in range(parts):
        for hop in hops:
            x_copy(0, hop, c).wait_recv()
            go(z_pass(hop, c))
    for hop in hops:
        to_sib(0, hop)
    z_copy(1).wait_recv()
    for hop in hops:
        go(x_pass(hop, 0))
    to_sib(3, 0)
    z_copy(0).wait_recv()
    to_sib(2, 0)
    for hop in hops:
        x_copy(1, hop, 0).wait_recv()
        to_sib(1, hop)

    pltpu.make_async_copy(lab.at[pl.ds(0, n - 1)], lab.at[pl.ds(0, n - 1)], lab_recv).wait()
    ones = jnp.sum(jnp.sum(lab[...].astype(jnp.float32), axis=0), keepdims=True)
    ones = jnp.broadcast_to(jnp.reshape(ones, (1, 1)), (1, LANES))
    w_one = -row_total / (2.0 * ones)
    w_zero = row_total / (2.0 * (row_total - ones))

    def weigh(row):
        return jnp.where(row == 1, w_one, w_zero)

    def part_weights(base, owner):
        def one(k, c):
            row = weigh(lab[owner * group + k, 0:1, :])
            w_part[base + k] = column(row, CP)
            return c
        lax.fori_loop(0, group, one, 0, unroll=small)

    load_m.wait()
    load_s.wait()
    w_rows = []
    for c in range(rows // LANES):
        row = weigh(lab[me, c : c + 1, :])
        w_rows.append(row)
        here = pl.ds(c * LANES, LANES)
        scaled[here, :] = (mul[here, :].astype(jnp.float32) * wide(column(row, LANES), cols)).astype(jnp.bfloat16)
    part_weights(0, blk)
    part_weights(group, prv)

    inv_band = 1.0 / jnp.broadcast_to(spread_v[...], (1, LANES))
    per = math.gcd(group, 4)
    take = per * CP

    def pairs(u_ref, m_ref, base, masked, first):
        def chunk(t, carry):
            boots, stat = carry
            some = pl.ds(t * per, per)
            u = u_ref[some].reshape(take, width)
            scores = lax.dot_general(u, unit[...], (((1,), (1,)), ((), ())), preferred_element_type=jnp.float32)
            kern = jnp.exp(scores * wide(inv_band, rows))
            if masked:
                at = lax.broadcasted_iota(jnp.int32, kern.shape, 0) + (t * per - slot) * CP
                lane = lax.broadcasted_iota(jnp.int32, kern.shape, 1)
                kern = jnp.where((at == lane) & (lane < CP), 0.0, kern)
            low = kern.astype(jnp.bfloat16)
            back = low.astype(jnp.float32)
            w = w_part[pl.ds(base + t * per, per)].reshape(take, LANES)
            signs = w.astype(jnp.bfloat16).astype(jnp.float32)
            total = back[:, :LANES] * w_rows[0]
            for c in range(1, rows // LANES):
                total = total + back[:, c * LANES : (c + 1) * LANES] * w_rows[c]
            stat = stat + jnp.sum(total * signs, axis=0, keepdims=True)
            new = []
            wide_cols = 2 * LANES
            for c in range(cols // wide_cols):
                here = pl.ds(c * wide_cols, wide_cols)
                mixed = jnp.dot(low, scaled[:, here], preferred_element_type=jnp.float32)
                m = m_ref[some, :, here].reshape(take, wide_cols).astype(jnp.float32)
                sc = (m * wide(w, wide_cols)).astype(jnp.bfloat16).astype(jnp.float32)
                new.append(boots[c] + jnp.sum(sc * mixed, axis=0, keepdims=True))
            return tuple(new), stat

        count = group // per
        if count == 1:
            return chunk(0, first)
        return lax.fori_loop(0, count, chunk, first)

    zero = (tuple(jnp.zeros((1, 2 * LANES), jnp.float32) for _ in range(cols // (2 * LANES))),
            jnp.zeros((1, LANES), jnp.float32))
    for hop in hops:
        x_pass(hop, 0).wait_recv()
        to_sib(3, hop)
    for c in range(parts):
        for hop in hops:
            z_pass(hop, c).wait_recv()
            to_sib(2, hop, c)
    from_sib(0)
    from_sib(1)
    acc = pairs(u_own, m_own, 0, True, zero)
    from_sib(2)
    from_sib(3)
    boots, stat = pairs(u_prev, m_prev, group, False, acc)

    for c, b in enumerate(boots):
        red[me, 2 * c : 2 * c + 1, :] = b[:, :LANES]
        red[me, 2 * c + 1 : 2 * c + 2, :] = b[:, LANES:]
    tiles = cols // LANES
    red[me, tiles : tiles + 1, :] = stat
    others(lambda d: remote(red.at[me], red.at[me], red_send, red_recv, d).start())
    for c in started:
        c.wait_send()
    pltpu.make_async_copy(lab.at[pl.ds(0, n - 1)], lab.at[pl.ds(0, n - 1)], lab_send).wait()
    pltpu.make_async_copy(red.at[pl.ds(0, n - 1)], red.at[pl.ds(0, n - 1)], red_recv).wait()
    pltpu.make_async_copy(red.at[pl.ds(0, n - 1)], red.at[pl.ds(0, n - 1)], red_send).wait()


def close(normalizer, red, boot_ref, stat_ref):
    total = jnp.sum(red[...], axis=0) * normalizer
    tiles = total.shape[0] - 1
    boot_ref[...] = total[:tiles]
    stat_ref[...] = jnp.sum(total[tiles:], axis=1, keepdims=True)


def body(sizes, embeddings, multipliers, labels, spread):
    n_blk, n_grp, n_sub = sizes
    group = n_grp * n_sub
    n = n_blk * group
    rows, width = embeddings.shape
    cols = multipliers.shape[1]
    bf16, f32 = jnp.bfloat16, jnp.float32
    dma = pltpu.SemaphoreType.DMA
    pieces = CP // PIECE
    red = pl.pallas_call(
        functools.partial(kernel, n_blk, n_grp, n_sub),
        out_shape=jax.ShapeDtypeStruct((n, cols // LANES + 1, LANES), f32),
        in_specs=[
            pl.BlockSpec(memory_space=pl.ANY),
            pl.BlockSpec(memory_space=pl.ANY),
            pl.BlockSpec(memory_space=pl.ANY),
            pl.BlockSpec(memory_space=pl.ANY),
        ],
        out_specs=pl.BlockSpec(memory_space=pltpu.VMEM),
        scratch_shapes=[
            pltpu.VMEM((rows, width), bf16),
            pltpu.VMEM((rows, cols), bf16),
            pltpu.VMEM((rows, width), bf16),
            pltpu.VMEM((rows, cols), bf16),
            pltpu.VMEM((group, CP, width), bf16),
            pltpu.VMEM((group, CP, width), bf16),
            pltpu.VMEM((group, CP, cols), bf16),
            pltpu.VMEM((group, CP, cols), bf16),
            pltpu.VMEM((n, rows // LANES, LANES), jnp.int32),
            pltpu.VMEM((2 * group, CP, LANES), f32),
            dma((6,)), dma, dma, dma, dma,
            dma((2, n_grp, pieces)), dma((2, n_grp, pieces)), dma((2,)), dma((2,)),
            dma((2, n_grp, pieces)), dma((2, n_grp, pieces)),
            dma((4, n_grp, n_sub, pieces)), dma((4, n_grp, n_sub, pieces)), pltpu.VMEM((1, 1), f32),
        ],
        compiler_params=pltpu.CompilerParams(
            collective_id=0, has_side_effects=True, vmem_limit_bytes=63 * 1024 * 1024
        ),
        name="bootstrap",
    )(spread.reshape(1, 1), labels.reshape(rows // LANES, LANES), embeddings, multipliers)
    normalizer = 1.0 / math.sqrt(float(n * rows) * 2 * group * CP)
    boot, stat = pl.pallas_call(
        functools.partial(close, normalizer),
        out_shape=(
            jax.ShapeDtypeStruct((cols // LANES, LANES), f32),
            jax.ShapeDtypeStruct((1, 1), f32),
        ),
        in_specs=[pl.BlockSpec(memory_space=pltpu.VMEM)],
        out_specs=(pl.BlockSpec(memory_space=pltpu.VMEM), pl.BlockSpec(memory_space=pltpu.VMEM)),
        name="close",
    )(red)
    return boot.reshape(cols), stat.reshape(1)


def solution(mesh):
    placed = (
        P(("feed", "blk", "grp", "sub"), None),
        P(("blk", "grp", "sub"), None),
        P(("feed", "blk", "grp", "sub")),
        P("feed"),
    )
    sizes = (mesh.shape["blk"], mesh.shape["grp"], mesh.shape["sub"])
    return jax.shard_map(
        functools.partial(body, sizes), mesh=mesh, in_specs=placed, out_specs=(P("feed"), P("feed")),
        check_vma=False,
    )
```

```python
import functools
import math

import jax
import jax.numpy as jnp
from jax import lax
from jax.experimental import pallas as pl
from jax.experimental.pallas import tpu as pltpu
from jax.sharding import PartitionSpec as P

CP = 48
LANES = 128
PIECE = 48
MESH = pl.DeviceIdType.MESH


def column(row, rows):
    return jnp.broadcast_to(row, (LANES, LANES)).T[:rows]


def wide(tile, width):
    return jnp.concatenate([tile] * (width // LANES), axis=1)


def kernel(
    n_blk, n_grp, n_sub, spread_ref, lab_hbm, emb_hbm, mul_hbm, red,
    emb, mul, unit, scaled, u_own, u_prev, m_own, m_prev, lab, w_part,
    load_sem, lab_send, lab_recv, red_send, red_recv,
    x_send, x_recv, z_send, z_recv, f_send, f_recv, s_send, s_recv, spread_v,
):
    feed, blk = lax.axis_index("feed"), lax.axis_index("blk")
    grp, sub = lax.axis_index("grp"), lax.axis_index("sub")
    group = n_grp * n_sub
    n = n_blk * group
    slot = grp * n_sub + sub
    me = blk * group + slot
    rows, width = emb.shape
    cols = mul.shape[1]
    row_total = float(n * rows)
    small = n <= 16
    nxt = lax.rem(blk + 1, n_blk)
    prv = lax.rem(blk + n_blk - 1, n_blk)

    def others(do):
        up = blk < n_blk // 2

        def one(b, lo):
            for k in range(lo, group):
                r = lax.rem(slot + k, group)
                do((feed, b, r // n_sub, lax.rem(r, n_sub)))

        def step(k, c):
            b = jnp.where(up, n_blk - 1 - k, k)
            past = jnp.where(up, b <= blk, b >= blk)
            one(jnp.where(past, jnp.where(up, b - 1, b + 1), b), 0)
            return c

        lax.fori_loop(0, n_blk - 1, step, 0, unroll=small)
        one(blk, 1)

    head_e = pltpu.make_async_copy(emb_hbm.at[pl.ds(0, CP)], emb.at[pl.ds(0, CP)], load_sem.at[0])
    head_m = pltpu.make_async_copy(mul_hbm.at[pl.ds(0, CP)], m_own.at[slot], load_sem.at[1])
    rest_e = pltpu.make_async_copy(
        emb_hbm.at[pl.ds(CP, rows - CP)], emb.at[pl.ds(CP, rows - CP)], load_sem.at[2])
    load_m = pltpu.make_async_copy(mul_hbm, mul, load_sem.at[3])
    load_l = pltpu.make_async_copy(lab_hbm, lab.at[me], load_sem.at[4])
    load_s = pltpu.make_async_copy(spread_ref, spread_v, load_sem.at[5])
    for c in (head_e, head_m, load_l, load_s, rest_e, load_m):
        c.start()

    barrier = pltpu.get_barrier_semaphore()
    others(lambda d: pl.semaphore_signal(barrier, inc=1, device_id=d, device_id_type=MESH))

    def normalise(lo, count):
        x = emb[pl.ds(lo, count), :].astype(jnp.float32)
        inv = lax.rsqrt(jnp.sum(x * x, axis=1, keepdims=True) + 1e-06)
        return (x * inv).astype(jnp.bfloat16)

    pl.semaphore_wait(barrier, n - 1)

    def remote(src, dst, send, recv, dev):
        return pltpu.make_async_remote_copy(
            src_ref=src, dst_ref=dst, send_sem=send, recv_sem=recv, device_id=dev, device_id_type=MESH)

    mul_head = mul_hbm.at[pl.ds(0, CP)]
    prev = (u_prev, m_prev)

    parts = CP // PIECE

    def piece(ref, at, c):
        return ref.at[at, pl.ds(c * PIECE, PIECE)]

    def x_copy(what, hop, c):
        src = piece(u_own, slot, c) if what == 0 else mul_head
        dst = piece(u_own, slot, c) if what == 0 else m_own.at[slot]
        return remote(src, dst, x_send.at[what, hop, c], x_recv.at[what, hop, c],
                      (feed, blk, lax.rem(grp + hop, n_grp), sub))

    def z_copy(what):
        return remote(u_own.at[slot] if what == 0 else mul_head, prev[what].at[slot], z_send.at[what], z_recv.at[what],
                      (feed, nxt, grp, sub))

    def behind(hop):
        return lax.rem(grp + n_grp - hop, n_grp)

    def z_pass(hop, c):
        at = behind(hop) * n_sub + sub
        return remote(piece(u_own, at, c), piece(u_prev, at, c), f_send.at[0, hop, c], f_recv.at[0, hop, c],
                      (feed, nxt, grp, sub))

    def x_pass(hop, c):
        return remote(m_prev.at[slot], m_prev.at[slot], f_send.at[1, hop, c], f_recv.at[1, hop, c],
                      (feed, blk, lax.rem(grp + hop, n_grp), sub))

    def sib(kind, hop, by, c):
        at = behind(hop) * n_sub + sub
        ref = refs[kind].at[at] if not split(kind, hop) else piece(refs[kind], at, c)
        return remote(ref, ref, s_send.at[kind, hop, by, c], s_recv.at[kind, hop, by, c],
                      (feed, blk, grp, lax.rem(sub + by, n_sub)))

    started = []

    def go(c):
        c.start()
        started.append(c)

    refs = (u_own, m_own, u_prev, m_prev)

    def split(kind, hop):
        return kind == 2 and hop > 0

    def to_sib(kind, hop, c=0):
        for by in range(1, n_sub):
            go(sib(kind, hop, by, c))

    def from_sib(kind):
        for hop in range(n_grp):
            for by in range(1, n_sub):
                for c in range(parts if split(kind, hop) else 1):
                    sib(kind, hop, by, c).wait_recv()

    hops = range(1, n_grp)
    go(z_copy(1))
    others(lambda d: remote(lab_hbm, lab.at[me], lab_send, lab_recv, d).start())
    head_e.wait()
    head = normalise(0, CP)
    u_own[slot] = head
    unit[pl.ds(0, CP), :] = head
    for c in range(parts):
        for hop in hops:
            go(x_copy(0, hop, c))
    go(z_copy(0))
    to_sib(0, 0)
    for hop in hops:
        go(x_copy(1, hop, 0))
    head_m.wait()
    to_sib(1, 0)

    rest_e.wait()
    step = 16 * ((rows - CP) // 64)
    for lo in range(CP, rows, step):
        count = min(step, rows - lo)
        unit[pl.ds(lo, count), :] = normalise(lo, count)

    for c in range(parts):
        for hop in hops:
            x_copy(0, hop, c).wait_recv()
            go(z_pass(hop, c))
    for hop in hops:
        to_sib(0, hop)
    z_copy(1).wait_recv()
    for hop in hops:
        go(x_pass(hop, 0))
    to_sib(3, 0)
    z_copy(0).wait_recv()
    to_sib(2, 0)
    for hop in hops:
        x_copy(1, hop, 0).wait_recv()
        to_sib(1, hop)

    load_l.wait()
    pltpu.make_async_copy(lab.at[pl.ds(0, n - 1)], lab.at[pl.ds(0, n - 1)], lab_recv).wait()
    ones = jnp.sum(jnp.sum(lab[...].astype(jnp.float32), axis=0), keepdims=True)
    ones = jnp.broadcast_to(jnp.reshape(ones, (1, 1)), (1, LANES))
    w_one = -row_total / (2.0 * ones)
    w_zero = row_total / (2.0 * (row_total - ones))

    def weigh(row):
        return jnp.where(row == 1, w_one, w_zero)

    def part_weights(base, owner):
        def one(k, c):
            row = weigh(lab[owner * group + k, 0:1, :])
            w_part[base + k] = column(row, CP)
            return c
        lax.fori_loop(0, group, one, 0, unroll=small)

    load_m.wait()
    load_s.wait()
    w_rows = []
    for c in range(rows // LANES):
        row = weigh(lab[me, c : c + 1, :])
        w_rows.append(row)
        here = pl.ds(c * LANES, LANES)
        scaled[here, :] = (mul[here, :].astype(jnp.float32) * wide(column(row, LANES), cols)).astype(jnp.bfloat16)
    part_weights(0, blk)
    part_weights(group, prv)

    inv_band = 1.0 / jnp.broadcast_to(spread_v[...], (1, LANES))
    per = math.gcd(group, 4)
    take = per * CP

    def pairs(u_ref, m_ref, base, masked, first):
        def chunk(t, carry):
            boots, stat = carry
            some = pl.ds(t * per, per)
            u = u_ref[some].reshape(take, width)
            scores = lax.dot_general(u, unit[...], (((1,), (1,)), ((), ())), preferred_element_type=jnp.float32)
            kern = jnp.exp(scores * wide(inv_band, rows))
            if masked:
                at = lax.broadcasted_iota(jnp.int32, kern.shape, 0) + (t * per - slot) * CP
                lane = lax.broadcasted_iota(jnp.int32, kern.shape, 1)
                kern = jnp.where((at == lane) & (lane < CP), 0.0, kern)
            low = kern.astype(jnp.bfloat16)
            back = low.astype(jnp.float32)
            w = w_part[pl.ds(base + t * per, per)].reshape(take, LANES)
            signs = w.astype(jnp.bfloat16).astype(jnp.float32)
            total = back[:, :LANES] * w_rows[0]
            for c in range(1, rows // LANES):
                total = total + back[:, c * LANES : (c + 1) * LANES] * w_rows[c]
            stat = stat + jnp.sum(total * signs, axis=0, keepdims=True)
            new = []
            wide_cols = 2 * LANES
            for c in range(cols // wide_cols):
                here = pl.ds(c * wide_cols, wide_cols)
                mixed = jnp.dot(low, scaled[:, here], preferred_element_type=jnp.float32)
                m = m_ref[some, :, here].reshape(take, wide_cols).astype(jnp.float32)
                sc = (m * wide(w, wide_cols)).astype(jnp.bfloat16).astype(jnp.float32)
                new.append(boots[c] + jnp.sum(sc * mixed, axis=0, keepdims=True))
            return tuple(new), stat

        count = group // per
        if count == 1:
            return chunk(0, first)
        return lax.fori_loop(0, count, chunk, first)

    zero = (tuple(jnp.zeros((1, 2 * LANES), jnp.float32) for _ in range(cols // (2 * LANES))),
            jnp.zeros((1, LANES), jnp.float32))
    for hop in hops:
        x_pass(hop, 0).wait_recv()
        to_sib(3, hop)
    for c in range(parts):
        for hop in hops:
            z_pass(hop, c).wait_recv()
            to_sib(2, hop, c)
    from_sib(0)
    from_sib(1)
    acc = pairs(u_own, m_own, 0, True, zero)
    from_sib(2)
    from_sib(3)
    boots, stat = pairs(u_prev, m_prev, group, False, acc)

    for c, b in enumerate(boots):
        red[me, 2 * c : 2 * c + 1, :] = b[:, :LANES]
        red[me, 2 * c + 1 : 2 * c + 2, :] = b[:, LANES:]
    tiles = cols // LANES
    red[me, tiles : tiles + 1, :] = stat
    others(lambda d: remote(red.at[me], red.at[me], red_send, red_recv, d).start())
    for c in started:
        c.wait_send()
    pltpu.make_async_copy(lab.at[pl.ds(0, n - 1)], lab.at[pl.ds(0, n - 1)], lab_send).wait()
    pltpu.make_async_copy(red.at[pl.ds(0, n - 1)], red.at[pl.ds(0, n - 1)], red_recv).wait()
    pltpu.make_async_copy(red.at[pl.ds(0, n - 1)], red.at[pl.ds(0, n - 1)], red_send).wait()


def close(normalizer, red, boot_ref, stat_ref):
    total = jnp.sum(red[...], axis=0) * normalizer
    tiles = total.shape[0] - 1
    boot_ref[...] = total[:tiles]
    stat_ref[...] = jnp.sum(total[tiles:], axis=1, keepdims=True)


def body(sizes, embeddings, multipliers, labels, spread):
    n_blk, n_grp, n_sub = sizes
    group = n_grp * n_sub
    n = n_blk * group
    rows, width = embeddings.shape
    cols = multipliers.shape[1]
    bf16, f32 = jnp.bfloat16, jnp.float32
    dma = pltpu.SemaphoreType.DMA
    pieces = CP // PIECE
    red = pl.pallas_call(
        functools.partial(kernel, n_blk, n_grp, n_sub),
        out_shape=jax.ShapeDtypeStruct((n, cols // LANES + 1, LANES), f32),
        in_specs=[
            pl.BlockSpec(memory_space=pl.ANY),
            pl.BlockSpec(memory_space=pl.ANY),
            pl.BlockSpec(memory_space=pl.ANY),
            pl.BlockSpec(memory_space=pl.ANY),
        ],
        out_specs=pl.BlockSpec(memory_space=pltpu.VMEM),
        scratch_shapes=[
            pltpu.VMEM((rows, width), bf16),
            pltpu.VMEM((rows, cols), bf16),
            pltpu.VMEM((rows, width), bf16),
            pltpu.VMEM((rows, cols), bf16),
            pltpu.VMEM((group, CP, width), bf16),
            pltpu.VMEM((group, CP, width), bf16),
            pltpu.VMEM((group, CP, cols), bf16),
            pltpu.VMEM((group, CP, cols), bf16),
            pltpu.VMEM((n, rows // LANES, LANES), jnp.int32),
            pltpu.VMEM((2 * group, CP, LANES), f32),
            dma((6,)), dma, dma, dma, dma,
            dma((2, n_grp, pieces)), dma((2, n_grp, pieces)), dma((2,)), dma((2,)),
            dma((2, n_grp, pieces)), dma((2, n_grp, pieces)),
            dma((4, n_grp, n_sub, pieces)), dma((4, n_grp, n_sub, pieces)), pltpu.VMEM((1, 1), f32),
        ],
        compiler_params=pltpu.CompilerParams(
            collective_id=0, has_side_effects=True, vmem_limit_bytes=63 * 1024 * 1024
        ),
        name="bootstrap",
    )(spread.reshape(1, 1), labels.reshape(rows // LANES, LANES), embeddings, multipliers)
    normalizer = 1.0 / math.sqrt(float(n * rows) * 2 * group * CP)
    boot, stat = pl.pallas_call(
        functools.partial(close, normalizer),
        out_shape=(
            jax.ShapeDtypeStruct((cols // LANES, LANES), f32),
            jax.ShapeDtypeStruct((1, 1), f32),
        ),
        in_specs=[pl.BlockSpec(memory_space=pltpu.VMEM)],
        out_specs=(pl.BlockSpec(memory_space=pltpu.VMEM), pl.BlockSpec(memory_space=pltpu.VMEM)),
        name="close",
    )(red)
    return boot.reshape(cols), stat.reshape(1)


def solution(mesh):
    placed = (
        P(("feed", "blk", "grp", "sub"), None),
        P(("blk", "grp", "sub"), None),
        P(("feed", "blk", "grp", "sub")),
        P("feed"),
    )
    sizes = (mesh.shape["blk"], mesh.shape["grp"], mesh.shape["sub"])
    return jax.shard_map(
        functools.partial(body, sizes), mesh=mesh, in_specs=placed, out_specs=(P("feed"), P("feed")),
        check_vma=False,
    )
```
